32 devices in a mesh: samp: 16 (over z, y, x), var: 2 (over core).
Axes of the slice: x: 2, y: 2, z: 4, core: 2. Of those that a mesh axis runs over, the one named last changes fastest.
Arguments:
- genotypes: bfloat16 [8192, 32768], P('samp', 'var'), may hold values from 0 to 2
- frequency: float32 [32768], P('var'), may hold values from 0.05 to 0.5
- start_block: float32 [32768, 16], P('var'), may hold values from -6 to 6
Outputs:
- loadings: float32 [32768, 16], P('var')
- scores: float32 [8192, 16], P('samp')
The draws below stay inside these ranges and needn't reach their ends.
All inputs are finite; a program needn't handle non-finite values.
Results may differ from the reference program's by a relative error of at most 0.013.
Values may be sent and summed in bfloat16 or wider, within the bound.
No kernel may reach another device: no remote copies, remote signals or barrier semaphores. Data moves between devices by JAX's collectives and lax.ppermute only.
A program may use at most 64 MiB of HBM per device.

```python
import jax
import jax.numpy as jnp
from jax import lax

SAMP_DEV = 512
VARIANTS = 32768
BLOCK = 16
ITERS = 2
SAMPLES = 8192
N_SAMP = 16
N_VAR = 2


def frequency_table(key):
    spread = jax.random.uniform(key, (VARIANTS,), jnp.float32, jnp.log(0.05), jnp.log(0.5))
    return jnp.clip(jnp.exp(spread), 0.05, 0.5)


def draw_frequency(key, part):
    return frequency_table(key)


def draw_genotypes(key, part):
    centre = 2.0 * frequency_table(key)
    key = jax.random.fold_in(key, 7)
    factor = jax.random.uniform(key, (SAMPLES, VARIANTS), jnp.float32, 0.0, 2.0)
    return jnp.clip(centre * factor, 0.0, 2.0).astype(jnp.bfloat16)


def block_levels(stream_key, shape, shards, low, largest):
    def one(position, blocks):
        draws = jax.random.uniform(jax.random.fold_in(jax.random.fold_in(stream_key, 6), position), (blocks,), jnp.float32, low / len(shards), largest / len(shards))
        return jnp.repeat(jnp.exp(draws), shape[position] // blocks).reshape((-1,) + (1,) * (len(shape) - position - 1))

    factor_of = one(*shards[0])
    for cut in shards[1:]:
        factor_of = factor_of * one(*cut)
    return factor_of


def scatter_about(rng, dims, deviation, most, shards=(), kind=jnp.bfloat16):
    result = deviation * jax.random.normal(rng, dims, jnp.float32)
    if shards:
        result = result * block_levels(rng, dims, shards, -0.22, 0.18)
    return jnp.clip(result, -most, most).astype(kind)


def setup_inputs(seed: int = 0) -> dict:
    splits = jax.random.split(jax.random.key(seed), 4)
    return {
        "genotypes": draw_genotypes(jax.random.fold_in(splits[3], 71), 0),
        "frequency": draw_frequency(jax.random.fold_in(splits[3], 71), 0),
        "start_block": scatter_about(splits[2], (VARIANTS, BLOCK), 1.0, 6.0, ((0, 2),), jnp.float32),
    }


def standardize(rows, frequency):
    centre = 2.0 * frequency
    return ((rows.astype(jnp.float32) - centre) / jnp.sqrt(centre * (1.0 - frequency))).astype(jnp.bfloat16)

def rounded_sample_side(scaled, narrow):
    width = VARIANTS // N_VAR
    left = scaled.astype(jnp.float32).reshape(scaled.shape[0], N_VAR, width)
    right = narrow.astype(jnp.float32).reshape(N_VAR, width, BLOCK)
    partial_terms = jnp.einsum('svk,vkb->svb', left, right)
    rounded = lax.optimization_barrier(partial_terms.astype(jnp.bfloat16))
    return lax.optimization_barrier(jnp.sum(rounded.astype(jnp.float32), axis=1)).astype(jnp.bfloat16)

def one_pass(genotypes, frequency, basis_cols):
    blocks = genotypes.reshape(N_SAMP, SAMP_DEV, VARIANTS)
    narrow = basis_cols.astype(jnp.bfloat16)

    def step_rows(total, rows):
        scaled = standardize(rows, frequency)
        sample_block = rounded_sample_side(scaled, narrow)
        total = total + jnp.dot(scaled.T.astype(jnp.float32), sample_block.astype(jnp.float32), preferred_element_type=jnp.float32)
        return (total, 0)
    total, unused = lax.scan(step_rows, jnp.zeros((VARIANTS, BLOCK), jnp.float32), blocks)
    return total

def score_pass(genotypes, frequency, basis_cols):
    blocks = genotypes.reshape(N_SAMP, SAMP_DEV, VARIANTS)
    narrow = basis_cols.astype(jnp.bfloat16)

    def step_rows(carry, rows):
        scaled = standardize(rows, frequency)
        return (carry, jnp.dot(scaled.astype(jnp.float32), narrow.astype(jnp.float32), preferred_element_type=jnp.float32))
    unused, pieces = lax.scan(step_rows, jnp.float32(0.0), blocks)
    return pieces.reshape(SAMP_DEV * N_SAMP, BLOCK)

def reference(genotypes, frequency, start_block):
    basis_cols = start_block
    for iteration in range(ITERS):
        variant_block = one_pass(genotypes, frequency, basis_cols)
        gram_matrix = jnp.dot(variant_block.T, variant_block, precision=lax.Precision.HIGHEST)
        factor = jnp.linalg.cholesky(gram_matrix)
        basis_cols = jax.scipy.linalg.solve_triangular(factor, variant_block.T, lower=True).T
    scores = score_pass(genotypes, frequency, basis_cols)
    loadings = basis_cols * jnp.sqrt(jnp.float32(VARIANTS))
    return (loadings, scores)
```

```python
import functools

import jax
import jax.numpy as jnp
from jax import lax
from jax.experimental import pallas as pl
from jax.experimental.pallas import tpu as pltpu
from jax.sharding import PartitionSpec as P

ITERS = 2
HALVES = 2
MIB = 1 << 20
LANES = 128
HERE = pl.BlockSpec(memory_space=pltpu.VMEM)
KEPT = pl.BlockSpec(memory_space=pltpu.VMEM)


def dot(a, b, over):
    return lax.dot_general(a, b, ((over[:1], over[1:]), ((), ())), preferred_element_type=jnp.float32)


def shape(dims, dtype=jnp.bfloat16):
    return jax.ShapeDtypeStruct(dims, dtype)


def call(body, out, operands, flops, name, vmem=4 * MIB):
    moved = sum(x.size * x.dtype.itemsize for x in operands)
    return pl.pallas_call(
        body,
        out_shape=out,
        in_specs=[HERE] * len(operands),
        out_specs=jax.tree.map(lambda _: HERE, out),
        compiler_params=pltpu.CompilerParams(vmem_limit_bytes=vmem),
        cost_estimate=pl.CostEstimate(flops=flops, bytes_accessed=moved, transcendentals=0),
        name=name,
    )(*operands)


def in_vmem(x):
    return pltpu.with_memory_space_constraint(x, pltpu.VMEM)


def in_hbm(x):
    return pltpu.with_memory_space_constraint(x, pltpu.HBM)


def in_parts(x, count):
    parts = []
    for _ in range(count):
        parts.append(x.astype(jnp.bfloat16).astype(jnp.float32))
        x = x - parts[-1]
    return parts


def load_body(width, group, g_ref, f_ref, b_ref, a_ref, t_ref, s_ref, centre_ref, root_ref, rows_ref, *scratch):
    f_vm, b_vm, inverse, parts, sems = scratch
    block = b_ref.shape[0]
    rows, cols = a_ref.shape
    steps = cols // width
    bodies = steps // group

    def columns(i, size):
        return pl.ds(pl.multiple_of(i * size, size), size)

    def chunk(i):
        here = columns(i, width)
        return pltpu.make_async_copy(g_ref.at[:, here], a_ref.at[:, here], sems.at[i])

    def start_chunk(i):
        here = columns(i, width * group)
        return pltpu.make_async_copy(b_ref.at[:, here], b_vm.at[:, here], sems.at[steps + 1 + i])

    table = pltpu.make_async_copy(f_ref, f_vm, sems.at[steps])
    table.start()

    @pl.loop(0, bodies)
    def _(i):
        start_chunk(i).start()
        for k in range(group):
            chunk(i * group + k).start()

    parts[...] = jnp.zeros(parts.shape, jnp.float32)
    table.wait()

    @pl.loop(0, f_vm.shape[0] // 8)
    def _(i):
        frequency = f_vm[columns(i, 8), :]
        centre = 2.0 * frequency
        root = jnp.sqrt(centre * (1.0 - frequency))
        scale = 1.0 / root
        high, middle, low = in_parts(centre, 3)
        for r in range(8):
            here = columns(8 * i + r, LANES)
            one = slice(r, r + 1)
            centre_ref[:, here] = centre[one]
            root_ref[:, here] = root[one]
            inverse[:, here] = scale[one]
            parts[0:1, here] = high[one]
            parts[1:2, here] = middle[one]
            parts[2:3, here] = low[one]

    def body(i, carry):
        total, shift = carry
        start_chunk(i).wait()
        for k in range(group):
            at = i * group + k
            here = columns(at, width)
            three = parts[:, here]
            three = jnp.concatenate([three, jnp.zeros_like(three)], axis=0).astype(jnp.bfloat16)
            rows_ref[:, here] = three
            narrow = (b_vm[:, here] * inverse[:, here]).astype(jnp.bfloat16)
            shift = shift + dot(narrow, three, (1, 1))
            chunk(at).wait()
            turned = a_ref[:, here].T
            t_ref[here, :] = turned
            total = total + dot(narrow, turned, (1, 0))
        return total, shift

    carry = (jnp.zeros((block, rows), jnp.float32), jnp.zeros((block, block), jnp.float32))
    total, shift = lax.fori_loop(0, bodies, body, carry)
    s_ref[...] = (total - jnp.sum(shift, axis=1, keepdims=True)).astype(jnp.bfloat16)


def load(genotypes, frequency, start_rows):
    rows, cols = genotypes.shape
    block = start_rows.shape[0]
    width = cols // 16
    anywhere = pl.BlockSpec(memory_space=pltpu.HBM)
    return pl.pallas_call(
        functools.partial(load_body, width, 8),
        in_specs=[anywhere] * 3,
        out_specs=[KEPT] * 2 + [HERE] * 4,
        out_shape=[
            pltpu.VMEM((rows, cols), jnp.bfloat16),
            pltpu.VMEM((cols, rows), jnp.bfloat16),
            shape((block, rows)),
            shape((1, cols), jnp.float32),
            shape((1, cols), jnp.float32),
            shape((block, cols)),
        ],
        scratch_shapes=[
            pltpu.VMEM((cols // LANES, LANES), jnp.float32),
            pltpu.VMEM((block, cols), jnp.float32),
            pltpu.VMEM((1, cols), jnp.float32),
            pltpu.VMEM((8, cols), jnp.float32),
            pltpu.SemaphoreType.DMA((cols // width + 3,)),
        ],
        compiler_params=pltpu.CompilerParams(vmem_limit_bytes=8 * MIB),
        name="load",
    )(in_hbm(genotypes), in_hbm(frequency.reshape(cols // LANES, LANES)), in_hbm(start_rows))


def columns_of(key, inner, width, cols):
    turn, half = key
    group = cols // inner
    place = lax.rem(lax.axis_index("samp"), inner) ^ turn
    return pl.ds(pl.multiple_of(place * group + (half or 0) * (group // HALVES), group // HALVES), width)


def terms_body(key, inner, centre_ref, a_ref, *refs):
    t_ref = refs[-1]
    columns = columns_of(key, inner, *(t_ref.shape[1], a_ref.shape[1]))
    rows = refs[0][...]
    if len(refs) == 3:
        rows = (rows.astype(jnp.float32) + refs[1][...].astype(jnp.float32)).astype(jnp.bfloat16)
    sums = jnp.sum(rows.astype(jnp.float32), axis=1, keepdims=True)
    t_ref[...] = (dot(rows, a_ref[:, columns], (1, 0)) - sums * centre_ref[:, columns]).astype(t_ref.dtype)


def terms(sample_rows, kept, centre, key, inner, dtype=jnp.bfloat16):
    width = kept.shape[1] // inner // (HALVES if key[1] is not None else 1)
    return call(
        functools.partial(terms_body, key, inner),
        shape((sample_rows[0].shape[0], width), dtype),
        (centre, in_vmem(kept), *sample_rows),
        10000,
        "terms%d%d" % (HALVES if key[1] is None else key[1], key[0]),
    )


def inner_sum_body(half, own_ref, *refs):
    value = own_ref[...]
    width = value.shape[1]
    for part in refs[:-1]:
        first = half * width if part.shape[1] > width else 0
        value = value + part[:, first : first + width].astype(jnp.float32)
    refs[-1][...] = value.astype(jnp.bfloat16)


def pair_sum_body(own_ref, other_ref, out_ref):
    out_ref[...] = (own_ref[...].astype(jnp.float32) + other_ref[...].astype(jnp.float32)).astype(jnp.bfloat16)


def outer_sum_body(key, inner, root_ref, own_ref, other_ref, out_ref):
    root = root_ref[:, columns_of(key, inner, out_ref.shape[1], root_ref.shape[1])]
    value = own_ref[...].astype(jnp.float32) + other_ref[...].astype(jnp.float32)
    out_ref[...] = (value / (root * root)).astype(jnp.bfloat16)


def stack_body(*refs):
    width = refs[0].shape[1]
    for k, part in enumerate(refs[:-1]):
        refs[-1][:, k * width : (k + 1) * width] = part[...]


def swap(x, axis, size, turn):
    return lax.ppermute(x, axis, [(d, d ^ turn) for d in range(size)])


def swap_across(x, size, turns_by_core):
    cores = len(turns_by_core)
    pairs = [(d * cores + v, (d ^ t) * cores + v) for d in range(size) for v, t in enumerate(turns_by_core)]
    return lax.ppermute(x, ("samp", "var"), pairs)


def sum_over_samples(sample_rows, kept, centre, root, inner):
    count, near, far = 4 * inner, inner, 2 * inner
    x, y, diagonal = 1, 2, 3
    across = swap(terms(sample_rows, kept, centre, (diagonal, None), inner), "samp", count, diagonal)
    pieces = {}
    for h in range(HALVES):
        received = [swap(terms(sample_rows, kept, centre, (t, h), inner), "samp", count, t) for t in (x, y)]
        own = terms(sample_rows, kept, centre, (0, h), inner, jnp.float32)
        piece = shape(own.shape)
        body = functools.partial(inner_sum_body, h)
        plane = call(body, piece, (own, *received, across), own.size * inner, "inner_sum%d" % h)
        pair = call(pair_sum_body, piece, (plane, swap_across(plane, count, (near, far))), own.size, "pair_sum%d" % h)
        body = functools.partial(outer_sum_body, (0, h), inner)
        whole = call(body, piece, (root, pair, swap_across(pair, count, (far, near))), own.size, "outer_sum%d" % h)
        pieces[0, h] = whole
        for t in (y, x):
            pieces[t, h] = swap(whole, "samp", count, t)
    both = [pieces[0, h] for h in range(HALVES)]
    group = shape((both[0].shape[0], HALVES * both[0].shape[1]))
    pieces[diagonal, None] = swap(call(stack_body, group, tuple(both), 0, "stack"), "samp", count, diagonal)
    order = [(0, 0), (y, 0), (x, 0), (0, 1), (diagonal, None), (y, 1), (x, 1)]
    return {key: pieces[key] for key in order}


def project_body(keys, inner, rows_ref, root_ref, turned_ref, *refs):
    pieces, out = refs[: len(keys)], refs[-1]
    block = pieces[0].shape[0]
    cols, rows = turned_ref.shape
    total = jnp.zeros((block, rows), jnp.float32)
    shift = jnp.zeros((block, block), jnp.float32)
    gram = jnp.zeros((block, block), jnp.float32)
    for key, piece in zip(keys, pieces):
        columns = columns_of(key, inner, piece.shape[1], cols)
        value = (piece[...].astype(jnp.float32) * root_ref[:, columns]).astype(jnp.bfloat16)
        gram += dot(value, value, (1, 1))
        shift += dot(piece[...], rows_ref[:, columns], (1, 1))
        total += dot(piece[...], turned_ref[columns, :], (1, 0))
    total -= jnp.sum(shift, axis=1, keepdims=True)
    gram = jnp.concatenate([gram, jnp.zeros((block, LANES - block), jnp.float32)], axis=1)
    if len(refs) == len(keys) + 2:
        total += refs[-2][:, :rows]
        gram += refs[-2][:, rows:]
    out[:, :rows] = total
    out[:, rows:] = gram


def project(pieces, turned, centre_rows, root, inner):
    order = list(pieces)
    block = centre_rows.shape[0]
    rows = turned.shape[1]
    total = ()
    for first, last in ((0, 4), (4, 5), (5, 6), (6, 7)):
        keys = order[first:last]
        operands = (centre_rows, root, in_vmem(turned), *(pieces[key] for key in keys)) + total
        body = functools.partial(project_body, keys, inner)
        out = shape((block, rows + LANES), jnp.float32)
        flops = (7 if first == 0 else 1) * 2 * rows * sum(pieces[key].size for key in keys)
        total = (call(body, out, operands, flops, "project%d" % first),)
    return total[0]


def inverse_factor(gram):
    block = gram.shape[0]
    dims = gram.shape
    row = lax.broadcasted_iota(jnp.int32, dims, 0)
    lane = lax.broadcasted_iota(jnp.int32, dims, 1)
    columns = [jnp.broadcast_to(gram[:, j : j + 1], dims) for j in range(block)]
    right = jnp.where(row == lane, 1.0, 0.0)
    scale = jnp.zeros(dims, jnp.float32)
    for k in range(block):
        pivot = jnp.broadcast_to(columns[k][k : k + 1], dims)
        factor = jnp.where(row > k, columns[k] / pivot, 0.0)
        scale = jnp.where(row == k, lax.rsqrt(pivot), scale)
        right = right - factor * jnp.broadcast_to(right[k : k + 1], dims)
        for j in range(k + 1, block):
            columns[j] = columns[j] - factor * jnp.broadcast_to(columns[j][k : k + 1], dims)
    return (right * scale)[:, :block]


def solve_both(own_ref, other_ref):
    rows = own_ref.shape[1] - LANES
    inverse = inverse_factor(own_ref[:, rows:] + other_ref[:, rows:])
    projected = lax.dot_general(
        inverse,
        own_ref[:, :rows] + other_ref[:, :rows],
        (((1,), (0,)), ((), ())),
        precision=lax.Precision.HIGHEST,
        preferred_element_type=jnp.float32,
    )
    return inverse, projected


def solve_body(own_ref, other_ref, out_ref):
    out_ref[...] = solve_both(own_ref, other_ref)[1].astype(out_ref.dtype)


def solve(own, other):
    block, rows = own.shape
    return call(solve_body, shape((block, rows - LANES)), (own, other), 6 * 32 * own.size, "solve")


def finish_body(scaling, order, inner, own_ref, other_ref, root_ref, *refs):
    pieces, (out, scores, held, kept_scores, sems) = refs[:-5], refs[-5:]
    block, cols = held.shape
    inverse, projected = solve_both(own_ref, other_ref)
    kept_scores[...] = projected
    copies = [pltpu.make_async_copy(kept_scores, scores, sems.at[len(order)])]
    copies[0].start()
    split = jnp.concatenate(in_parts(inverse * scaling, 2), axis=0).astype(jnp.bfloat16)
    done = 0
    for at, (key, piece) in enumerate(zip(order, pieces)):
        width = piece.shape[1]
        columns = columns_of(key, inner, width, cols)
        value = dot(split, piece[...], (1, 0))
        here = slice(done, done + width)
        held[:, here] = (value[:block] + value[block:]) * root_ref[:, columns]
        copies.append(pltpu.make_async_copy(held.at[:, here], out.at[:, columns], sems.at[at]))
        copies[-1].start()
        done += width
    for copy in copies:
        copy.wait()


def finish(own, other, root, pieces, scaling, inner):
    block, cols = own.shape[0], root.shape[1]
    rows = own.shape[1] - LANES
    order = list(pieces)
    return pl.pallas_call(
        functools.partial(finish_body, scaling, order, inner),
        out_shape=[shape((block, cols), jnp.float32), shape((block, rows), jnp.float32)],
        in_specs=[HERE] * (3 + len(order)),
        out_specs=[pl.BlockSpec(memory_space=pltpu.HBM)] * 2,
        scratch_shapes=[
            pltpu.VMEM((block, cols), jnp.float32),
            pltpu.VMEM((block, rows), jnp.float32),
            pltpu.SemaphoreType.DMA((len(order) + 1,)),
        ],
        compiler_params=pltpu.CompilerParams(vmem_limit_bytes=8 * MIB),
        name="finish",
    )(own, other, root, *pieces.values())


def make_local(inner, var):
    def local(genotypes, frequency, start_block):
        scaling = float(start_block.shape[0] * var) ** 0.5
        kept, turned, own, centre, root, centre_rows = load(genotypes, frequency, start_block.T)
        sample_rows = (own, swap(own, "var", var, 1))
        for iteration in range(ITERS):
            pieces = sum_over_samples(sample_rows, kept, centre, root, inner)
            own = project(pieces, turned, centre_rows, root, inner)
            other = swap(own, "var", var, 1)
            if iteration < ITERS - 1:
                sample_rows = (solve(own, other),)
        loadings, scores = finish(own, other, root, pieces, scaling, inner)
        return loadings.T, scores.T

    return local


def dot_plain(a, b, dims, **kw):
    return lax.dot_general(a, b, (dims, ((), ())), preferred_element_type=jnp.float32, **kw)


def make_plain(samp, var):
    def local(genotypes, frequency, start_block):
        block = start_block.shape[1]
        centre = 2.0 * frequency
        kept = ((genotypes.astype(jnp.float32) - centre) / jnp.sqrt(centre * (1.0 - frequency))).astype(jnp.bfloat16)
        narrow = start_block.astype(jnp.bfloat16).T
        sample_rows = lax.psum(dot_plain(narrow, kept, ((1,), (1,))).astype(jnp.bfloat16), "var")
        for iteration in range(ITERS):
            rows = dot_plain(sample_rows.astype(jnp.bfloat16), kept, ((1,), (0,)))
            rows = lax.psum(rows, "samp").astype(jnp.bfloat16)
            gram = lax.psum(dot_plain(rows, rows, ((1,), (1,))), "var")
            factor = jnp.linalg.cholesky(gram)
            eye = jnp.eye(block, dtype=jnp.float32)
            inverse = jax.scipy.linalg.solve_triangular(factor, eye, lower=True)
            projected = lax.psum(dot_plain(rows, kept, ((1,), (1,))), "var")
            high = lax.Precision.HIGHEST
            sample_rows = dot_plain(inverse, projected, ((1,), (0,)), precision=high)
        scaling = float(start_block.shape[0] * var) ** 0.5
        loadings = dot_plain(inverse * scaling, rows.astype(jnp.float32), ((1,), (0,)), precision=high)
        return loadings.T, sample_rows.T

    return local


def solution(mesh):
    samp, var = mesh.shape["samp"], mesh.shape["var"]

    def whole(genotypes, frequency, start_block):
        cols = start_block.shape[0] // var
        if samp == 16 and var == 2 and cols % (samp * LANES) == 0:
            local = make_local(samp // 4, var)
        else:
            local = make_plain(samp, var)
        placed = (P("samp", "var"), P("var"), P("var", None))
        return jax.shard_map(
            local, mesh=mesh, in_specs=placed, out_specs=(P("var", None), P("samp", None)), check_vma=False
        )(genotypes, frequency, start_block)

    return whole
```

```python
import functools

import jax
import jax.numpy as jnp
from jax import lax
from jax.experimental import pallas as pl
from jax.experimental.pallas import tpu as pltpu
from jax.sharding import PartitionSpec as P

ITERS = 2
HALVES = 2
MIB = 1 << 20
LANES = 128
HERE = pl.BlockSpec(memory_space=pltpu.VMEM)
KEPT = pl.BlockSpec(memory_space=pltpu.VMEM)


def dot(a, b, over):
    return lax.dot_general(a, b, ((over[:1], over[1:]), ((), ())), preferred_element_type=jnp.float32)


def shape(dims, dtype=jnp.bfloat16):
    return jax.ShapeDtypeStruct(dims, dtype)


def call(body, out, operands, flops, name, vmem=4 * MIB):
    moved = sum(x.size * x.dtype.itemsize for x in operands)
    return pl.pallas_call(
        body,
        out_shape=out,
        in_specs=[HERE] * len(operands),
        out_specs=jax.tree.map(lambda _: HERE, out),
        compiler_params=pltpu.CompilerParams(vmem_limit_bytes=vmem),
        cost_estimate=pl.CostEstimate(flops=flops, bytes_accessed=moved, transcendentals=0),
        name=name,
    )(*operands)


def in_vmem(x):
    return pltpu.with_memory_space_constraint(x, pltpu.VMEM)


def in_hbm(x):
    return pltpu.with_memory_space_constraint(x, pltpu.HBM)


def in_parts(x, count):
    parts = []
    for _ in range(count):
        parts.append(x.astype(jnp.bfloat16).astype(jnp.float32))
        x = x - parts[-1]
    return parts


def load_body(width, group, g_ref, f_ref, b_ref, a_ref, t_ref, s_ref, centre_ref, root_ref, rows_ref, *scratch):
    f_vm, b_vm, inverse, parts, sems = scratch
    block = b_ref.shape[0]
    rows, cols = a_ref.shape
    steps = cols // width
    bodies = steps // group

    def columns(i, size):
        return pl.ds(pl.multiple_of(i * size, size), size)

    def chunk(i):
        here = columns(i, width)
        return pltpu.make_async_copy(g_ref.at[:, here], a_ref.at[:, here], sems.at[i])

    def start_chunk(i):
        here = columns(i, width * group)
        return pltpu.make_async_copy(b_ref.at[:, here], b_vm.at[:, here], sems.at[steps + 1 + i])

    table = pltpu.make_async_copy(f_ref, f_vm, sems.at[steps])
    table.start()

    @pl.loop(0, bodies)
    def _(i):
        start_chunk(i).start()
        for k in range(group):
            chunk(i * group + k).start()

    parts[...] = jnp.zeros(parts.shape, jnp.float32)
    table.wait()

    @pl.loop(0, f_vm.shape[0] // 8)
    def _(i):
        frequency = f_vm[columns(i, 8), :]
        centre = 2.0 * frequency
        root = jnp.sqrt(centre * (1.0 - frequency))
        scale = 1.0 / root
        high, middle, low = in_parts(centre, 3)
        for r in range(8):
            here = columns(8 * i + r, LANES)
            one = slice(r, r + 1)
            centre_ref[:, here] = centre[one]
            root_ref[:, here] = root[one]
            inverse[:, here] = scale[one]
            parts[0:1, here] = high[one]
            parts[1:2, here] = middle[one]
            parts[2:3, here] = low[one]

    def body(i, carry):
        total, shift = carry
        start_chunk(i).wait()
        for k in range(group):
            at = i * group + k
            here = columns(at, width)
            three = parts[:, here]
            three = jnp.concatenate([three, jnp.zeros_like(three)], axis=0).astype(jnp.bfloat16)
            rows_ref[:, here] = three
            narrow = (b_vm[:, here] * inverse[:, here]).astype(jnp.bfloat16)
            shift = shift + dot(narrow, three, (1, 1))
            chunk(at).wait()
            turned = a_ref[:, here].T
            t_ref[here, :] = turned
            total = total + dot(narrow, turned, (1, 0))
        return total, shift

    carry = (jnp.zeros((block, rows), jnp.float32), jnp.zeros((block, block), jnp.float32))
    total, shift = lax.fori_loop(0, bodies, body, carry)
    s_ref[...] = (total - jnp.sum(shift, axis=1, keepdims=True)).astype(jnp.bfloat16)


def load(genotypes, frequency, start_rows):
    rows, cols = genotypes.shape
    block = start_rows.shape[0]
    width = cols // 16
    anywhere = pl.BlockSpec(memory_space=pltpu.HBM)
    return pl.pallas_call(
        functools.partial(load_body, width, 8),
        in_specs=[anywhere] * 3,
        out_specs=[KEPT] * 2 + [HERE] * 4,
        out_shape=[
            pltpu.VMEM((rows, cols), jnp.bfloat16),
            pltpu.VMEM((cols, rows), jnp.bfloat16),
            shape((block, rows)),
            shape((1, cols), jnp.float32),
            shape((1, cols), jnp.float32),
            shape((block, cols)),
        ],
        scratch_shapes=[
            pltpu.VMEM((cols // LANES, LANES), jnp.float32),
            pltpu.VMEM((block, cols), jnp.float32),
            pltpu.VMEM((1, cols), jnp.float32),
            pltpu.VMEM((8, cols), jnp.float32),
            pltpu.SemaphoreType.DMA((cols // width + 3,)),
        ],
        compiler_params=pltpu.CompilerParams(vmem_limit_bytes=8 * MIB),
        name="load",
    )(in_hbm(genotypes), in_hbm(frequency.reshape(cols // LANES, LANES)), in_hbm(start_rows))


def columns_of(key, inner, width, cols):
    turn, half = key
    group = cols // inner
    place = lax.rem(lax.axis_index("samp"), inner) ^ turn
    return pl.ds(pl.multiple_of(place * group + (half or 0) * (group // HALVES), group // HALVES), width)


def terms_body(key, inner, centre_ref, a_ref, *refs):
    t_ref = refs[-1]
    columns = columns_of(key, inner, *(t_ref.shape[1], a_ref.shape[1]))
    rows = refs[0][...]
    if len(refs) == 3:
        rows = (rows.astype(jnp.float32) + refs[1][...].astype(jnp.float32)).astype(jnp.bfloat16)
    sums = jnp.sum(rows.astype(jnp.float32), axis=1, keepdims=True)
    t_ref[...] = (dot(rows, a_ref[:, columns], (1, 0)) - sums * centre_ref[:, columns]).astype(t_ref.dtype)


def terms(sample_rows, kept, centre, key, inner, dtype=jnp.bfloat16):
    width = kept.shape[1] // inner // (HALVES if key[1] is not None else 1)
    return call(
        functools.partial(terms_body, key, inner),
        shape((sample_rows[0].shape[0], width), dtype),
        (centre, in_vmem(kept), *sample_rows),
        10000,
        "terms%d%d" % (HALVES if key[1] is None else key[1], key[0]),
    )


def inner_sum_body(half, own_ref, *refs):
    value = own_ref[...]
    width = value.shape[1]
    for part in refs[:-1]:
        first = half * width if part.shape[1] > width else 0
        value = value + part[:, first : first + width].astype(jnp.float32)
    refs[-1][...] = value.astype(jnp.bfloat16)


def pair_sum_body(own_ref, other_ref, out_ref):
    out_ref[...] = (own_ref[...].astype(jnp.float32) + other_ref[...].astype(jnp.float32)).astype(jnp.bfloat16)


def outer_sum_body(key, inner, root_ref, own_ref, other_ref, out_ref):
    root = root_ref[:, columns_of(key, inner, out_ref.shape[1], root_ref.shape[1])]
    value = own_ref[...].astype(jnp.float32) + other_ref[...].astype(jnp.float32)
    out_ref[...] = (value / (root * root)).astype(jnp.bfloat16)


def stack_body(*refs):
    width = refs[0].shape[1]
    for k, part in enumerate(refs[:-1]):
        refs[-1][:, k * width : (k + 1) * width] = part[...]


def swap(x, axis, size, turn):
    return lax.ppermute(x, axis, [(d, d ^ turn) for d in range(size)])


def swap_across(x, size, turns_by_core):
    cores = len(turns_by_core)
    pairs = [(d * cores + v, (d ^ t) * cores + v) for d in range(size) for v, t in enumerate(turns_by_core)]
    return lax.ppermute(x, ("samp", "var"), pairs)


def sum_over_samples(sample_rows, kept, centre, root, inner):
    count, near, far = 4 * inner, inner, 2 * inner
    x, y, diagonal = 1, 2, 3
    across = [swap(terms(sample_rows, kept, centre, (t, None), inner), "samp", count, t) for t in (diagonal, y)]
    pieces = {}
    for h in range(HALVES):
        beside = swap(terms(sample_rows, kept, centre, (x, h), inner), "samp", count, x)
        own = terms(sample_rows, kept, centre, (0, h), inner, jnp.float32)
        piece = shape(own.shape)
        body = functools.partial(inner_sum_body, h)
        plane = call(body, piece, (own, beside, *across[::-1]), own.size * inner, "inner_sum%d" % h)
        pair = call(pair_sum_body, piece, (plane, swap_across(plane, count, (near, far))), own.size, "pair_sum%d" % h)
        body = functools.partial(outer_sum_body, (0, h), inner)
        whole = call(body, piece, (root, pair, swap_across(pair, count, (far, near))), own.size, "outer_sum%d" % h)
        pieces[0, h] = whole
        for t in (y, x):
            pieces[t, h] = swap(whole, "samp", count, t)
    both = [pieces[0, h] for h in range(HALVES)]
    group = shape((both[0].shape[0], HALVES * both[0].shape[1]))
    pieces[diagonal, None] = swap(call(stack_body, group, tuple(both), 0, "stack"), "samp", count, diagonal)
    order = [(0, 0), (y, 0), (x, 0), (0, 1), (diagonal, None), (y, 1), (x, 1)]
    return {key: pieces[key] for key in order}


def project_body(keys, inner, rows_ref, root_ref, turned_ref, *refs):
    pieces, out = refs[: len(keys)], refs[-1]
    block = pieces[0].shape[0]
    cols, rows = turned_ref.shape
    total = jnp.zeros((block, rows), jnp.float32)
    shift = jnp.zeros((block, block), jnp.float32)
    gram = jnp.zeros((block, block), jnp.float32)
    for key, piece in zip(keys, pieces):
        columns = columns_of(key, inner, piece.shape[1], cols)
        value = (piece[...].astype(jnp.float32) * root_ref[:, columns]).astype(jnp.bfloat16)
        gram += dot(value, value, (1, 1))
        shift += dot(piece[...], rows_ref[:, columns], (1, 1))
        total += dot(piece[...], turned_ref[columns, :], (1, 0))
    total -= jnp.sum(shift, axis=1, keepdims=True)
    gram = jnp.concatenate([gram, jnp.zeros((block, LANES - block), jnp.float32)], axis=1)
    if len(refs) == len(keys) + 2:
        total += refs[-2][:, :rows]
        gram += refs[-2][:, rows:]
    out[:, :rows] = total
    out[:, rows:] = gram


def project(pieces, turned, centre_rows, root, inner):
    order = list(pieces)
    block = centre_rows.shape[0]
    rows = turned.shape[1]
    total = ()
    for first, last in ((0, 4), (4, 5), (5, 6), (6, 7)):
        keys = order[first:last]
        operands = (centre_rows, root, in_vmem(turned), *(pieces[key] for key in keys)) + total
        body = functools.partial(project_body, keys, inner)
        out = shape((block, rows + LANES), jnp.float32)
        flops = (7 if first == 0 else 1) * 2 * rows * sum(pieces[key].size for key in keys)
        total = (call(body, out, operands, flops, "project%d" % first),)
    return total[0]


def inverse_factor(gram):
    block = gram.shape[0]
    dims = gram.shape
    row = lax.broadcasted_iota(jnp.int32, dims, 0)
    lane = lax.broadcasted_iota(jnp.int32, dims, 1)
    columns = [jnp.broadcast_to(gram[:, j : j + 1], dims) for j in range(block)]
    right = jnp.where(row == lane, 1.0, 0.0)
    scale = jnp.zeros(dims, jnp.float32)
    for k in range(block):
        pivot = jnp.broadcast_to(columns[k][k : k + 1], dims)
        factor = jnp.where(row > k, columns[k] / pivot, 0.0)
        scale = jnp.where(row == k, lax.rsqrt(pivot), scale)
        right = right - factor * jnp.broadcast_to(right[k : k + 1], dims)
        for j in range(k + 1, block):
            columns[j] = columns[j] - factor * jnp.broadcast_to(columns[j][k : k + 1], dims)
    return (right * scale)[:, :block]


def solve_both(own_ref, other_ref):
    rows = own_ref.shape[1] - LANES
    inverse = inverse_factor(own_ref[:, rows:] + other_ref[:, rows:])
    projected = lax.dot_general(
        inverse,
        own_ref[:, :rows] + other_ref[:, :rows],
        (((1,), (0,)), ((), ())),
        precision=lax.Precision.HIGHEST,
        preferred_element_type=jnp.float32,
    )
    return inverse, projected


def solve_body(own_ref, other_ref, out_ref):
    out_ref[...] = solve_both(own_ref, other_ref)[1].astype(out_ref.dtype)


def solve(own, other):
    block, rows = own.shape
    return call(solve_body, shape((block, rows - LANES)), (own, other), 6 * 32 * own.size, "solve")


def finish_body(scaling, order, inner, own_ref, other_ref, root_ref, *refs):
    pieces, (out, scores, held, kept_scores, sems) = refs[:-5], refs[-5:]
    block, cols = held.shape
    inverse, projected = solve_both(own_ref, other_ref)
    kept_scores[...] = projected
    copies = [pltpu.make_async_copy(kept_scores, scores, sems.at[len(order)])]
    copies[0].start()
    split = jnp.concatenate(in_parts(inverse * scaling, 2), axis=0).astype(jnp.bfloat16)
    done = 0
    for at, (key, piece) in enumerate(zip(order, pieces)):
        width = piece.shape[1]
        columns = columns_of(key, inner, width, cols)
        value = dot(split, piece[...], (1, 0))
        here = slice(done, done + width)
        held[:, here] = (value[:block] + value[block:]) * root_ref[:, columns]
        copies.append(pltpu.make_async_copy(held.at[:, here], out.at[:, columns], sems.at[at]))
        copies[-1].start()
        done += width
    for copy in copies:
        copy.wait()


def finish(own, other, root, pieces, scaling, inner):
    block, cols = own.shape[0], root.shape[1]
    rows = own.shape[1] - LANES
    order = list(pieces)
    return pl.pallas_call(
        functools.partial(finish_body, scaling, order, inner),
        out_shape=[shape((block, cols), jnp.float32), shape((block, rows), jnp.float32)],
        in_specs=[HERE] * (3 + len(order)),
        out_specs=[pl.BlockSpec(memory_space=pltpu.HBM)] * 2,
        scratch_shapes=[
            pltpu.VMEM((block, cols), jnp.float32),
            pltpu.VMEM((block, rows), jnp.float32),
            pltpu.SemaphoreType.DMA((len(order) + 1,)),
        ],
        compiler_params=pltpu.CompilerParams(vmem_limit_bytes=8 * MIB),
        name="finish",
    )(own, other, root, *pieces.values())


def make_local(inner, var):
    def local(genotypes, frequency, start_block):
        scaling = float(start_block.shape[0] * var) ** 0.5
        kept, turned, own, centre, root, centre_rows = load(genotypes, frequency, start_block.T)
        sample_rows = (own, swap(own, "var", var, 1))
        for iteration in range(ITERS):
            pieces = sum_over_samples(sample_rows, kept, centre, root, inner)
            own = project(pieces, turned, centre_rows, root, inner)
            other = swap(own, "var", var, 1)
            if iteration < ITERS - 1:
                sample_rows = (solve(own, other),)
        loadings, scores = finish(own, other, root, pieces, scaling, inner)
        return loadings.T, scores.T

    return local


def dot_plain(a, b, dims, **kw):
    return lax.dot_general(a, b, (dims, ((), ())), preferred_element_type=jnp.float32, **kw)


def make_plain(samp, var):
    def local(genotypes, frequency, start_block):
        block = start_block.shape[1]
        centre = 2.0 * frequency
        kept = ((genotypes.astype(jnp.float32) - centre) / jnp.sqrt(centre * (1.0 - frequency))).astype(jnp.bfloat16)
        narrow = start_block.astype(jnp.bfloat16).T
        sample_rows = lax.psum(dot_plain(narrow, kept, ((1,), (1,))).astype(jnp.bfloat16), "var")
        for iteration in range(ITERS):
            rows = dot_plain(sample_rows.astype(jnp.bfloat16), kept, ((1,), (0,)))
            rows = lax.psum(rows, "samp").astype(jnp.bfloat16)
            gram = lax.psum(dot_plain(rows, rows, ((1,), (1,))), "var")
            factor = jnp.linalg.cholesky(gram)
            eye = jnp.eye(block, dtype=jnp.float32)
            inverse = jax.scipy.linalg.solve_triangular(factor, eye, lower=True)
            projected = lax.psum(dot_plain(rows, kept, ((1,), (1,))), "var")
            high = lax.Precision.HIGHEST
            sample_rows = dot_plain(inverse, projected, ((1,), (0,)), precision=high)
        scaling = float(start_block.shape[0] * var) ** 0.5
        loadings = dot_plain(inverse * scaling, rows.astype(jnp.float32), ((1,), (0,)), precision=high)
        return loadings.T, sample_rows.T

    return local


def solution(mesh):
    samp, var = mesh.shape["samp"], mesh.shape["var"]

    def whole(genotypes, frequency, start_block):
        cols = start_block.shape[0] // var
        if samp == 16 and var == 2 and cols % (samp * LANES) == 0:
            local = make_local(samp // 4, var)
        else:
            local = make_plain(samp, var)
        placed = (P("samp", "var"), P("var"), P("var", None))
        return jax.shard_map(
            local, mesh=mesh, in_specs=placed, out_specs=(P("var", None), P("samp", None)), check_vma=False
        )(genotypes, frequency, start_block)

    return whole
```

```python
import functools

import jax
import jax.numpy as jnp
from jax import lax
from jax.experimental import pallas as pl
from jax.experimental.pallas import tpu as pltpu
from jax.sharding import PartitionSpec as P

ITERS = 2
HALVES = 2
MIB = 1 << 20
LANES = 128
HERE = pl.BlockSpec(memory_space=pltpu.VMEM)
KEPT = pl.BlockSpec(memory_space=pltpu.VMEM)


def dot(a, b, over):
    return lax.dot_general(a, b, ((over[:1], over[1:]), ((), ())), preferred_element_type=jnp.float32)


def shape(dims, dtype=jnp.bfloat16):
    return jax.ShapeDtypeStruct(dims, dtype)


def call(body, out, operands, flops, name, vmem=4 * MIB):
    moved = sum(x.size * x.dtype.itemsize for x in operands)
    return pl.pallas_call(
        body,
        out_shape=out,
        in_specs=[HERE] * len(operands),
        out_specs=jax.tree.map(lambda _: HERE, out),
        compiler_params=pltpu.CompilerParams(vmem_limit_bytes=vmem),
        cost_estimate=pl.CostEstimate(flops=flops, bytes_accessed=moved, transcendentals=0),
        name=name,
    )(*operands)


def in_vmem(x):
    return pltpu.with_memory_space_constraint(x, pltpu.VMEM)


def in_hbm(x):
    return pltpu.with_memory_space_constraint(x, pltpu.HBM)


def in_parts(x, count):
    parts = []
    for _ in range(count):
        parts.append(x.astype(jnp.bfloat16).astype(jnp.float32))
        x = x - parts[-1]
    return parts


def centred(narrow, centre):
    terms = narrow.astype(jnp.float32) * centre
    total = terms[:, :LANES]
    for first in range(LANES, terms.shape[1], LANES):
        total = total + terms[:, first : first + LANES]
    return total


def load_body(width, group, g_ref, f_ref, b_ref, a_ref, t_ref, s_ref, centre_ref, root_ref, *scratch):
    f_vm, b_vm, inverse, sems = scratch
    block = b_ref.shape[0]
    rows, cols = a_ref.shape
    steps = cols // width
    bodies = steps // group

    def columns(i, size):
        return pl.ds(pl.multiple_of(i * size, size), size)

    def chunk(i):
        here = columns(i, width)
        return pltpu.make_async_copy(g_ref.at[:, here], a_ref.at[:, here], sems.at[i])

    def start_chunk(i):
        here = columns(i, width * group)
        return pltpu.make_async_copy(b_ref.at[:, here], b_vm.at[:, here], sems.at[steps + 1 + i])

    table = pltpu.make_async_copy(f_ref, f_vm, sems.at[steps])
    table.start()

    @pl.loop(0, bodies)
    def _(i):
        start_chunk(i).start()
        for k in range(group):
            chunk(i * group + k).start()

    table.wait()

    @pl.loop(0, f_vm.shape[0] // 8)
    def _(i):
        frequency = f_vm[columns(i, 8), :]
        centre = 2.0 * frequency
        root = jnp.sqrt(centre * (1.0 - frequency))
        scale = 1.0 / root
        for r in range(8):
            here = columns(8 * i + r, LANES)
            one = slice(r, r + 1)
            centre_ref[:, here] = centre[one]
            root_ref[:, here] = root[one]
            inverse[:, here] = scale[one]

    def body(i, carry):
        total, shift = carry
        start_chunk(i).wait()
        for k in range(group):
            at = i * group + k
            here = columns(at, width)
            narrow = (b_vm[:, here] * inverse[:, here]).astype(jnp.bfloat16)
            shift = shift + centred(narrow, centre_ref[:, here])
            chunk(at).wait()
            turned = a_ref[:, here].T
            t_ref[here, :] = turned
            total = total + dot(narrow, turned, (1, 0))
        return total, shift

    carry = (jnp.zeros((block, rows), jnp.float32), jnp.zeros((block, LANES), jnp.float32))
    total, shift = lax.fori_loop(0, bodies, body, carry)
    s_ref[...] = (total - jnp.sum(shift, axis=1, keepdims=True)).astype(jnp.bfloat16)


def load(genotypes, frequency, start_rows):
    rows, cols = genotypes.shape
    block = start_rows.shape[0]
    width = cols // 16
    anywhere = pl.BlockSpec(memory_space=pltpu.HBM)
    return pl.pallas_call(
        functools.partial(load_body, width, 8),
        in_specs=[anywhere] * 3,
        out_specs=[KEPT] * 2 + [HERE] * 3,
        out_shape=[
            pltpu.VMEM((rows, cols), jnp.bfloat16),
            pltpu.VMEM((cols, rows), jnp.bfloat16),
            shape((block, rows)),
            shape((1, cols), jnp.float32),
            shape((1, cols), jnp.float32),
        ],
        scratch_shapes=[
            pltpu.VMEM((cols // LANES, LANES), jnp.float32),
            pltpu.VMEM((block, cols), jnp.float32),
            pltpu.VMEM((1, cols), jnp.float32),
            pltpu.SemaphoreType.DMA((cols // width + 3,)),
        ],
        compiler_params=pltpu.CompilerParams(vmem_limit_bytes=8 * MIB),
        name="load",
    )(in_hbm(genotypes), in_hbm(frequency.reshape(cols // LANES, LANES)), in_hbm(start_rows))


def columns_of(key, inner, width, cols):
    turn, half = key
    group = cols // inner
    place = lax.rem(lax.axis_index("samp"), inner) ^ turn
    return pl.ds(pl.multiple_of(place * group + (half or 0) * (group // HALVES), group // HALVES), width)


def terms_body(key, inner, centre_ref, a_ref, *refs):
    t_ref = refs[-1]
    columns = columns_of(key, inner, *(t_ref.shape[1], a_ref.shape[1]))
    rows = refs[0][...]
    if len(refs) == 3:
        rows = (rows.astype(jnp.float32) + refs[1][...].astype(jnp.float32)).astype(jnp.bfloat16)
    sums = jnp.sum(rows.astype(jnp.float32), axis=1, keepdims=True)
    t_ref[...] = (dot(rows, a_ref[:, columns], (1, 0)) - sums * centre_ref[:, columns]).astype(t_ref.dtype)


def terms(sample_rows, kept, centre, key, inner, dtype=jnp.bfloat16):
    width = kept.shape[1] // inner // (HALVES if key[1] is not None else 1)
    return call(
        functools.partial(terms_body, key, inner),
        shape((sample_rows[0].shape[0], width), dtype),
        (centre, in_vmem(kept), *sample_rows),
        10000,
        "terms%d%d" % (HALVES if key[1] is None else key[1], key[0]),
    )


def inner_sum_body(half, own_ref, *refs):
    value = own_ref[...]
    width = value.shape[1]
    for part in refs[:-1]:
        first = half * width if part.shape[1] > width else 0
        value = value + part[:, first : first + width].astype(jnp.float32)
    refs[-1][...] = value.astype(jnp.bfloat16)


def pair_sum_body(own_ref, other_ref, out_ref):
    out_ref[...] = (own_ref[...].astype(jnp.float32) + other_ref[...].astype(jnp.float32)).astype(jnp.bfloat16)


def outer_sum_body(key, inner, root_ref, own_ref, other_ref, out_ref):
    root = root_ref[:, columns_of(key, inner, out_ref.shape[1], root_ref.shape[1])]
    value = own_ref[...].astype(jnp.float32) + other_ref[...].astype(jnp.float32)
    out_ref[...] = (value / (root * root)).astype(jnp.bfloat16)


def stack_body(*refs):
    width = refs[0].shape[1]
    for k, part in enumerate(refs[:-1]):
        refs[-1][:, k * width : (k + 1) * width] = part[...]


def swap(x, axis, size, turn):
    return lax.ppermute(x, axis, [(d, d ^ turn) for d in range(size)])


def swap_across(x, size, turns_by_core):
    cores = len(turns_by_core)
    pairs = [(d * cores + v, (d ^ t) * cores + v) for d in range(size) for v, t in enumerate(turns_by_core)]
    return lax.ppermute(x, ("samp", "var"), pairs)


def sum_over_samples(sample_rows, kept, centre, root, inner):
    count, near, far = 4 * inner, inner, 2 * inner
    x, y, diagonal = 1, 2, 3
    across = swap(terms(sample_rows, kept, centre, (diagonal, None), inner), "samp", count, diagonal)
    pieces = {}
    for h in range(HALVES):
        received = [swap(terms(sample_rows, kept, centre, (t, h), inner), "samp", count, t) for t in (x, y)]
        own = terms(sample_rows, kept, centre, (0, h), inner, jnp.float32)
        piece = shape(own.shape)
        body = functools.partial(inner_sum_body, h)
        plane = call(body, piece, (own, *received, across), own.size * inner, "inner_sum%d" % h)
        pair = call(pair_sum_body, piece, (plane, swap_across(plane, count, (near, far))), own.size, "pair_sum%d" % h)
        body = functools.partial(outer_sum_body, (0, h), inner)
        whole = call(body, piece, (root, pair, swap_across(pair, count, (far, near))), own.size, "outer_sum%d" % h)
        pieces[0, h] = whole
        for t in (y, x):
            pieces[t, h] = swap(whole, "samp", count, t)
    both = [pieces[0, h] for h in range(HALVES)]
    group = shape((both[0].shape[0], HALVES * both[0].shape[1]))
    pieces[diagonal, None] = swap(call(stack_body, group, tuple(both), 0, "stack"), "samp", count, diagonal)
    order = [(0, 0), (y, 0), (x, 0), (0, 1), (diagonal, None), (y, 1), (x, 1)]
    return {key: pieces[key] for key in order}


def project_body(keys, inner, centre_ref, root_ref, turned_ref, *refs):
    pieces, out = refs[: len(keys)], refs[-1]
    block = pieces[0].shape[0]
    cols, rows = turned_ref.shape
    total = jnp.zeros((block, rows), jnp.float32)
    shift = jnp.zeros((block, LANES), jnp.float32)
    gram = jnp.zeros((block, block), jnp.float32)
    for key, piece in zip(keys, pieces):
        columns = columns_of(key, inner, piece.shape[1], cols)
        value = (piece[...].astype(jnp.float32) * root_ref[:, columns]).astype(jnp.bfloat16)
        gram += dot(value, value, (1, 1))
        shift += centred(piece[...], centre_ref[:, columns])
        total += dot(piece[...], turned_ref[columns, :], (1, 0))
    total -= jnp.sum(shift, axis=1, keepdims=True)
    gram = jnp.concatenate([gram, jnp.zeros((block, LANES - block), jnp.float32)], axis=1)
    if len(refs) == len(keys) + 2:
        total += refs[-2][:, :rows]
        gram += refs[-2][:, rows:]
    out[:, :rows] = total
    out[:, rows:] = gram


def project(pieces, turned, centre, root, inner):
    order = list(pieces)
    block = pieces[0, 0].shape[0]
    rows = turned.shape[1]
    total = ()
    for first, last in ((0, 4), (4, 5), (5, 6), (6, 7)):
        keys = order[first:last]
        operands = (centre, root, in_vmem(turned), *(pieces[key] for key in keys)) + total
        body = functools.partial(project_body, keys, inner)
        out = shape((block, rows + LANES), jnp.float32)
        flops = (7 if first == 0 else 1) * 2 * rows * sum(pieces[key].size for key in keys)
        total = (call(body, out, operands, flops, "project%d" % first),)
    return total[0]


def inverse_factor(gram):
    block = gram.shape[0]
    dims = gram.shape
    row = lax.broadcasted_iota(jnp.int32, dims, 0)
    lane = lax.broadcasted_iota(jnp.int32, dims, 1)
    columns = [jnp.broadcast_to(gram[:, j : j + 1], dims) for j in range(block)]
    right = jnp.where(row == lane, 1.0, 0.0)
    scale = jnp.zeros(dims, jnp.float32)
    for k in range(block):
        pivot = jnp.broadcast_to(columns[k][k : k + 1], dims)
        factor = jnp.where(row > k, columns[k] / pivot, 0.0)
        scale = jnp.where(row == k, lax.rsqrt(pivot), scale)
        right = right - factor * jnp.broadcast_to(right[k : k + 1], dims)
        for j in range(k + 1, block):
            columns[j] = columns[j] - factor * jnp.broadcast_to(columns[j][k : k + 1], dims)
    return (right * scale)[:, :block]


def solve_both(own_ref, other_ref):
    rows = own_ref.shape[1] - LANES
    inverse = inverse_factor(own_ref[:, rows:] + other_ref[:, rows:])
    projected = lax.dot_general(
        inverse,
        own_ref[:, :rows] + other_ref[:, :rows],
        (((1,), (0,)), ((), ())),
        precision=lax.Precision.HIGHEST,
        preferred_element_type=jnp.float32,
    )
    return inverse, projected


def solve_body(own_ref, other_ref, out_ref):
    out_ref[...] = solve_both(own_ref, other_ref)[1].astype(out_ref.dtype)


def solve(own, other):
    block, rows = own.shape
    return call(solve_body, shape((block, rows - LANES)), (own, other), 6 * 32 * own.size, "solve")


def finish_body(scaling, order, inner, own_ref, other_ref, root_ref, *refs):
    pieces, (out, scores, held, kept_scores, sems) = refs[:-5], refs[-5:]
    block, cols = held.shape
    inverse, projected = solve_both(own_ref, other_ref)
    kept_scores[...] = projected
    copies = [pltpu.make_async_copy(kept_scores, scores, sems.at[len(order)])]
    copies[0].start()
    split = jnp.concatenate(in_parts(inverse * scaling, 2), axis=0).astype(jnp.bfloat16)
    done = 0
    for at, (key, piece) in enumerate(zip(order, pieces)):
        width = piece.shape[1]
        columns = columns_of(key, inner, width, cols)
        value = dot(split, piece[...], (1, 0))
        here = slice(done, done + width)
        held[:, here] = (value[:block] + value[block:]) * root_ref[:, columns]
        copies.append(pltpu.make_async_copy(held.at[:, here], out.at[:, columns], sems.at[at]))
        copies[-1].start()
        done += width
    for copy in copies:
        copy.wait()


def finish(own, other, root, pieces, scaling, inner):
    block, cols = own.shape[0], root.shape[1]
    rows = own.shape[1] - LANES
    order = list(pieces)
    return pl.pallas_call(
        functools.partial(finish_body, scaling, order, inner),
        out_shape=[shape((block, cols), jnp.float32), shape((block, rows), jnp.float32)],
        in_specs=[HERE] * (3 + len(order)),
        out_specs=[pl.BlockSpec(memory_space=pltpu.HBM)] * 2,
        scratch_shapes=[
            pltpu.VMEM((block, cols), jnp.float32),
            pltpu.VMEM((block, rows), jnp.float32),
            pltpu.SemaphoreType.DMA((len(order) + 1,)),
        ],
        compiler_params=pltpu.CompilerParams(vmem_limit_bytes=8 * MIB),
        name="finish",
    )(own, other, root, *pieces.values())


def make_local(inner, var):
    def local(genotypes, frequency, start_block):
        scaling = float(start_block.shape[0] * var) ** 0.5
        kept, turned, own, centre, root = load(genotypes, frequency, start_block.T)
        sample_rows = (own, swap(own, "var", var, 1))
        for iteration in range(ITERS):
            pieces = sum_over_samples(sample_rows, kept, centre, root, inner)
            own = project(pieces, turned, centre, root, inner)
            other = swap(own, "var", var, 1)
            if iteration < ITERS - 1:
                sample_rows = (solve(own, other),)
        loadings, scores = finish(own, other, root, pieces, scaling, inner)
        return loadings.T, scores.T

    return local


def dot_plain(a, b, dims, **kw):
    return lax.dot_general(a, b, (dims, ((), ())), preferred_element_type=jnp.float32, **kw)


def make_plain(samp, var):
    def local(genotypes, frequency, start_block):
        block = start_block.shape[1]
        centre = 2.0 * frequency
        kept = ((genotypes.astype(jnp.float32) - centre) / jnp.sqrt(centre * (1.0 - frequency))).astype(jnp.bfloat16)
        narrow = start_block.astype(jnp.bfloat16).T
        sample_rows = lax.psum(dot_plain(narrow, kept, ((1,), (1,))).astype(jnp.bfloat16), "var")
        for iteration in range(ITERS):
            rows = dot_plain(sample_rows.astype(jnp.bfloat16), kept, ((1,), (0,)))
            rows = lax.psum(rows, "samp").astype(jnp.bfloat16)
            gram = lax.psum(dot_plain(rows, rows, ((1,), (1,))), "var")
            factor = jnp.linalg.cholesky(gram)
            eye = jnp.eye(block, dtype=jnp.float32)
            inverse = jax.scipy.linalg.solve_triangular(factor, eye, lower=True)
            projected = lax.psum(dot_plain(rows, kept, ((1,), (1,))), "var")
            high = lax.Precision.HIGHEST
            sample_rows = dot_plain(inverse, projected, ((1,), (0,)), precision=high)
        scaling = float(start_block.shape[0] * var) ** 0.5
        loadings = dot_plain(inverse * scaling, rows.astype(jnp.float32), ((1,), (0,)), precision=high)
        return loadings.T, sample_rows.T

    return local


def solution(mesh):
    samp, var = mesh.shape["samp"], mesh.shape["var"]

    def whole(genotypes, frequency, start_block):
        cols = start_block.shape[0] // var
        if samp == 16 and var == 2 and cols % (samp * LANES) == 0:
            local = make_local(samp // 4, var)
        else:
            local = make_plain(samp, var)
        placed = (P("samp", "var"), P("var"), P("var", None))
        return jax.shard_map(
            local, mesh=mesh, in_specs=placed, out_specs=(P("var", None), P("samp", None)), check_vma=False
        )(genotypes, frequency, start_block)

    return whole
```

```python
import functools

import jax
import jax.numpy as jnp
from jax import lax
from jax.experimental import pallas as pl
from jax.experimental.pallas import tpu as pltpu
from jax.sharding import PartitionSpec as P

ITERS = 2
HALVES = 2
DIAGONAL, SIDE, OTHER_SIDE = 3, 4, 5
MIB = 1 << 20
LANES = 128
HERE = pl.BlockSpec(memory_space=pltpu.VMEM)
KEPT = pl.BlockSpec(memory_space=pltpu.VMEM)


def dot(a, b, over):
    return lax.dot_general(a, b, ((over[:1], over[1:]), ((), ())), preferred_element_type=jnp.float32)


def shape(dims, dtype=jnp.bfloat16):
    return jax.ShapeDtypeStruct(dims, dtype)


def call(body, out, operands, flops, name, vmem=4 * MIB):
    moved = sum(x.size * x.dtype.itemsize for x in operands)
    return pl.pallas_call(
        body,
        out_shape=out,
        in_specs=[HERE] * len(operands),
        out_specs=jax.tree.map(lambda _: HERE, out),
        compiler_params=pltpu.CompilerParams(vmem_limit_bytes=vmem),
        cost_estimate=pl.CostEstimate(flops=flops, bytes_accessed=moved, transcendentals=0),
        name=name,
    )(*operands)


def in_vmem(x):
    return pltpu.with_memory_space_constraint(x, pltpu.VMEM)


def in_hbm(x):
    return pltpu.with_memory_space_constraint(x, pltpu.HBM)


def in_parts(x, count):
    parts = []
    for _ in range(count):
        parts.append(x.astype(jnp.bfloat16).astype(jnp.float32))
        x = x - parts[-1]
    return parts


def centred(narrow, centre):
    terms = narrow.astype(jnp.float32) * centre
    total = terms[:, :LANES]
    for first in range(LANES, terms.shape[1], LANES):
        total = total + terms[:, first : first + LANES]
    return total


def load_body(width, group, g_ref, f_ref, b_ref, a_ref, t_ref, s_ref, centre_ref, root_ref, *scratch):
    f_vm, b_vm, inverse, sems = scratch
    block = b_ref.shape[0]
    rows, cols = a_ref.shape
    steps = cols // width
    bodies = steps // group

    def columns(i, size):
        return pl.ds(pl.multiple_of(i * size, size), size)

    def chunk(i):
        here = columns(i, width)
        return pltpu.make_async_copy(g_ref.at[:, here], a_ref.at[:, here], sems.at[i])

    def start_chunk(i):
        here = columns(i, width * group)
        return pltpu.make_async_copy(b_ref.at[:, here], b_vm.at[:, here], sems.at[steps + 1 + i])

    table = pltpu.make_async_copy(f_ref, f_vm, sems.at[steps])
    table.start()

    @pl.loop(0, bodies)
    def _(i):
        start_chunk(i).start()
        for k in range(group):
            chunk(i * group + k).start()

    table.wait()

    @pl.loop(0, f_vm.shape[0] // 8)
    def _(i):
        frequency = f_vm[columns(i, 8), :]
        centre = 2.0 * frequency
        root = jnp.sqrt(centre * (1.0 - frequency))
        scale = 1.0 / root
        for r in range(8):
            here = columns(8 * i + r, LANES)
            one = slice(r, r + 1)
            centre_ref[:, here] = centre[one]
            root_ref[:, here] = root[one]
            inverse[:, here] = scale[one]

    def body(i, carry):
        total, shift = carry
        start_chunk(i).wait()
        for k in range(group):
            at = i * group + k
            here = columns(at, width)
            narrow = (b_vm[:, here] * inverse[:, here]).astype(jnp.bfloat16)
            shift = shift + centred(narrow, centre_ref[:, here])
            chunk(at).wait()
            turned = a_ref[:, here].T
            t_ref[here, :] = turned
            total = total + dot(narrow, turned, (1, 0))
        return total, shift

    carry = (jnp.zeros((block, rows), jnp.float32), jnp.zeros((block, LANES), jnp.float32))
    total, shift = lax.fori_loop(0, bodies, body, carry)
    s_ref[...] = (total - jnp.sum(shift, axis=1, keepdims=True)).astype(jnp.bfloat16)


def load(genotypes, frequency, start_rows):
    rows, cols = genotypes.shape
    block = start_rows.shape[0]
    width = cols // 16
    anywhere = pl.BlockSpec(memory_space=pltpu.HBM)
    return pl.pallas_call(
        functools.partial(load_body, width, 8),
        in_specs=[anywhere] * 3,
        out_specs=[KEPT] * 2 + [HERE] * 3,
        out_shape=[
            pltpu.VMEM((rows, cols), jnp.bfloat16),
            pltpu.VMEM((cols, rows), jnp.bfloat16),
            shape((block, rows)),
            shape((1, cols), jnp.float32),
            shape((1, cols), jnp.float32),
        ],
        scratch_shapes=[
            pltpu.VMEM((cols // LANES, LANES), jnp.float32),
            pltpu.VMEM((block, cols), jnp.float32),
            pltpu.VMEM((1, cols), jnp.float32),
            pltpu.SemaphoreType.DMA((cols // width + 3,)),
        ],
        compiler_params=pltpu.CompilerParams(vmem_limit_bytes=8 * MIB),
        name="load",
    )(in_hbm(genotypes), in_hbm(frequency.reshape(cols // LANES, LANES)), in_hbm(start_rows))


def columns_of(key, inner, width, cols):
    turn, half = key
    core = lax.axis_index("var")
    turn = {SIDE: 2 - core, OTHER_SIDE: 1 + core}.get(turn, turn)
    group = cols // inner
    place = lax.rem(lax.axis_index("samp"), inner) ^ turn
    return pl.ds(pl.multiple_of(place * group + (half or 0) * (group // HALVES), group // HALVES), width)


def terms_body(key, inner, centre_ref, a_ref, *refs):
    t_ref = refs[-1]
    columns = columns_of(key, inner, *(t_ref.shape[1], a_ref.shape[1]))
    rows = refs[0][...]
    if len(refs) == 3:
        rows = (rows.astype(jnp.float32) + refs[1][...].astype(jnp.float32)).astype(jnp.bfloat16)
    sums = jnp.sum(rows.astype(jnp.float32), axis=1, keepdims=True)
    t_ref[...] = (dot(rows, a_ref[:, columns], (1, 0)) - sums * centre_ref[:, columns]).astype(t_ref.dtype)


def terms(sample_rows, kept, centre, key, inner, dtype=jnp.bfloat16):
    width = kept.shape[1] // inner // (HALVES if key[1] is not None else 1)
    return call(
        functools.partial(terms_body, key, inner),
        shape((sample_rows[0].shape[0], width), dtype),
        (centre, in_vmem(kept), *sample_rows),
        10000,
        "terms%d%d" % (HALVES if key[1] is None else key[1], key[0]),
    )


def inner_sum_body(half, own_ref, *refs):
    value = own_ref[...]
    width = value.shape[1]
    for part in refs[:-1]:
        first = half * width if part.shape[1] > width else 0
        value = value + part[:, first : first + width].astype(jnp.float32)
    refs[-1][...] = value.astype(jnp.bfloat16)


def pair_sum_body(own_ref, other_ref, out_ref):
    out_ref[...] = (own_ref[...].astype(jnp.float32) + other_ref[...].astype(jnp.float32)).astype(jnp.bfloat16)


def outer_sum_body(key, inner, root_ref, own_ref, other_ref, out_ref):
    root = root_ref[:, columns_of(key, inner, out_ref.shape[1], root_ref.shape[1])]
    value = own_ref[...].astype(jnp.float32) + other_ref[...].astype(jnp.float32)
    out_ref[...] = (value / (root * root)).astype(jnp.bfloat16)


def stack_body(*refs):
    width = refs[0].shape[1]
    for k, part in enumerate(refs[:-1]):
        refs[-1][:, k * width : (k + 1) * width] = part[...]


def swap(x, axis, size, turn):
    return lax.ppermute(x, axis, [(d, d ^ turn) for d in range(size)])


def swap_across(x, size, turns_by_core):
    cores = len(turns_by_core)
    pairs = [(d * cores + v, (d ^ t) * cores + v) for d in range(size) for v, t in enumerate(turns_by_core)]
    return lax.ppermute(x, ("samp", "var"), pairs)


def sum_over_samples(sample_rows, kept, centre, root, inner):
    count, near, far = 4 * inner, inner, 2 * inner
    meet = {DIAGONAL: (3, 3), SIDE: (2, 1), OTHER_SIDE: (1, 2)}
    across = swap_across(terms(sample_rows, kept, centre, (DIAGONAL, None), inner), count, meet[DIAGONAL])
    pieces = {}
    for h in range(HALVES):
        sides = OTHER_SIDE, SIDE
        received = [swap_across(terms(sample_rows, kept, centre, (t, h), inner), count, meet[t]) for t in sides]
        own = terms(sample_rows, kept, centre, (0, h), inner, jnp.float32)
        piece = shape(own.shape)
        body = functools.partial(inner_sum_body, h)
        plane = call(body, piece, (own, *received, across), own.size * inner, "inner_sum%d" % h)
        pair = call(pair_sum_body, piece, (plane, swap_across(plane, count, (near, far))), own.size, "pair_sum%d" % h)
        body = functools.partial(outer_sum_body, (0, h), inner)
        whole = call(body, piece, (root, pair, swap_across(pair, count, (far, near))), own.size, "outer_sum%d" % h)
        pieces[0, h] = whole
        for t in (SIDE, OTHER_SIDE):
            pieces[t, h] = swap_across(whole, count, meet[t])
    both = [pieces[0, h] for h in range(HALVES)]
    group = shape((both[0].shape[0], HALVES * both[0].shape[1]))
    pieces[DIAGONAL, None] = swap_across(call(stack_body, group, tuple(both), 0, "stack"), count, meet[DIAGONAL])
    order = [(0, 0), (SIDE, 0), (OTHER_SIDE, 0), (0, 1), (DIAGONAL, None), (SIDE, 1), (OTHER_SIDE, 1)]
    return {key: pieces[key] for key in order}


def project_body(keys, inner, centre_ref, root_ref, turned_ref, *refs):
    pieces, out = refs[: len(keys)], refs[-1]
    block = pieces[0].shape[0]
    cols, rows = turned_ref.shape
    total = jnp.zeros((block, rows), jnp.float32)
    shift = jnp.zeros((block, LANES), jnp.float32)
    gram = jnp.zeros((block, block), jnp.float32)
    for key, piece in zip(keys, pieces):
        columns = columns_of(key, inner, piece.shape[1], cols)
        value = (piece[...].astype(jnp.float32) * root_ref[:, columns]).astype(jnp.bfloat16)
        gram += dot(value, value, (1, 1))
        shift += centred(piece[...], centre_ref[:, columns])
        total += dot(piece[...], turned_ref[columns, :], (1, 0))
    total -= jnp.sum(shift, axis=1, keepdims=True)
    gram = jnp.concatenate([gram, jnp.zeros((block, LANES - block), jnp.float32)], axis=1)
    if len(refs) == len(keys) + 2:
        total += refs[-2][:, :rows]
        gram += refs[-2][:, rows:]
    out[:, :rows] = total
    out[:, rows:] = gram


def project(pieces, turned, centre, root, inner):
    order = list(pieces)
    block = pieces[0, 0].shape[0]
    rows = turned.shape[1]
    total = ()
    for first, last in ((0, 4), (4, 5), (5, 6), (6, 7)):
        keys = order[first:last]
        operands = (centre, root, in_vmem(turned), *(pieces[key] for key in keys)) + total
        body = functools.partial(project_body, keys, inner)
        out = shape((block, rows + LANES), jnp.float32)
        flops = (7 if first == 0 else 1) * 2 * rows * sum(pieces[key].size for key in keys)
        total = (call(body, out, operands, flops, "project%d" % first),)
    return total[0]


def inverse_factor(gram):
    block = gram.shape[0]
    dims = gram.shape
    row = lax.broadcasted_iota(jnp.int32, dims, 0)
    lane = lax.broadcasted_iota(jnp.int32, dims, 1)
    columns = [jnp.broadcast_to(gram[:, j : j + 1], dims) for j in range(block)]
    right = jnp.where(row == lane, 1.0, 0.0)
    scale = jnp.zeros(dims, jnp.float32)
    for k in range(block):
        pivot = jnp.broadcast_to(columns[k][k : k + 1], dims)
        factor = jnp.where(row > k, columns[k] / pivot, 0.0)
        scale = jnp.where(row == k, lax.rsqrt(pivot), scale)
        right = right - factor * jnp.broadcast_to(right[k : k + 1], dims)
        for j in range(k + 1, block):
            columns[j] = columns[j] - factor * jnp.broadcast_to(columns[j][k : k + 1], dims)
    return (right * scale)[:, :block]


def inverse_of(own_ref, other_ref):
    rows = own_ref.shape[1] - LANES
    return inverse_factor(own_ref[:, rows:] + other_ref[:, rows:])


def applied(inverse, own_ref, other_ref):
    rows = own_ref.shape[1] - LANES
    return lax.dot_general(
        inverse,
        own_ref[:, :rows] + other_ref[:, :rows],
        (((1,), (0,)), ((), ())),
        precision=lax.Precision.HIGHEST,
        preferred_element_type=jnp.float32,
    )


def solve_body(own_ref, other_ref, out_ref):
    out_ref[...] = applied(inverse_of(own_ref, other_ref), own_ref, other_ref).astype(out_ref.dtype)


def solve(own, other):
    block, rows = own.shape
    return call(solve_body, shape((block, rows - LANES)), (own, other), 6 * 32 * own.size, "solve")


def finish_body(scaling, order, inner, own_ref, other_ref, root_ref, *refs):
    pieces, (out, scores, held, kept_scores, sems) = refs[:-5], refs[-5:]
    block, cols = held.shape
    inverse = inverse_of(own_ref, other_ref)
    copies = []
    split = jnp.concatenate(in_parts(inverse * scaling, 2), axis=0).astype(jnp.bfloat16)
    done = 0
    for at, (key, piece) in enumerate(zip(order, pieces)):
        width = piece.shape[1]
        columns = columns_of(key, inner, width, cols)
        value = dot(split, piece[...], (1, 0))
        here = slice(done, done + width)
        held[:, here] = (value[:block] + value[block:]) * root_ref[:, columns]
        copies.append(pltpu.make_async_copy(held.at[:, here], out.at[:, columns], sems.at[at]))
        copies[-1].start()
        done += width
    kept_scores[...] = applied(inverse, own_ref, other_ref)
    copies.append(pltpu.make_async_copy(kept_scores, scores, sems.at[len(order)]))
    copies[-1].start()
    for copy in copies:
        copy.wait()


def finish(own, other, root, pieces, scaling, inner):
    block, cols = own.shape[0], root.shape[1]
    rows = own.shape[1] - LANES
    order = list(pieces)
    return pl.pallas_call(
        functools.partial(finish_body, scaling, order, inner),
        out_shape=[shape((block, cols), jnp.float32), shape((block, rows), jnp.float32)],
        in_specs=[HERE] * (3 + len(order)),
        out_specs=[pl.BlockSpec(memory_space=pltpu.HBM)] * 2,
        scratch_shapes=[
            pltpu.VMEM((block, cols), jnp.float32),
            pltpu.VMEM((block, rows), jnp.float32),
            pltpu.SemaphoreType.DMA((len(order) + 1,)),
        ],
        compiler_params=pltpu.CompilerParams(vmem_limit_bytes=8 * MIB),
        name="finish",
    )(own, other, root, *pieces.values())


def make_local(inner, var):
    def local(genotypes, frequency, start_block):
        scaling = float(start_block.shape[0] * var) ** 0.5
        kept, turned, own, centre, root = load(genotypes, frequency, start_block.T)
        sample_rows = (own, swap(own, "var", var, 1))
        for iteration in range(ITERS):
            pieces = sum_over_samples(sample_rows, kept, centre, root, inner)
            own = project(pieces, turned, centre, root, inner)
            other = swap(own, "var", var, 1)
            if iteration < ITERS - 1:
                sample_rows = (solve(own, other),)
        loadings, scores = finish(own, other, root, pieces, scaling, inner)
        return loadings.T, scores.T

    return local


def dot_plain(a, b, dims, **kw):
    return lax.dot_general(a, b, (dims, ((), ())), preferred_element_type=jnp.float32, **kw)


def make_plain(samp, var):
    def local(genotypes, frequency, start_block):
        block = start_block.shape[1]
        centre = 2.0 * frequency
        kept = ((genotypes.astype(jnp.float32) - centre) / jnp.sqrt(centre * (1.0 - frequency))).astype(jnp.bfloat16)
        narrow = start_block.astype(jnp.bfloat16).T
        sample_rows = lax.psum(dot_plain(narrow, kept, ((1,), (1,))).astype(jnp.bfloat16), "var")
        for iteration in range(ITERS):
            rows = dot_plain(sample_rows.astype(jnp.bfloat16), kept, ((1,), (0,)))
            rows = lax.psum(rows, "samp").astype(jnp.bfloat16)
            gram = lax.psum(dot_plain(rows, rows, ((1,), (1,))), "var")
            factor = jnp.linalg.cholesky(gram)
            eye = jnp.eye(block, dtype=jnp.float32)
            inverse = jax.scipy.linalg.solve_triangular(factor, eye, lower=True)
            projected = lax.psum(dot_plain(rows, kept, ((1,), (1,))), "var")
            high = lax.Precision.HIGHEST
            sample_rows = dot_plain(inverse, projected, ((1,), (0,)), precision=high)
        scaling = float(start_block.shape[0] * var) ** 0.5
        loadings = dot_plain(inverse * scaling, rows.astype(jnp.float32), ((1,), (0,)), precision=high)
        return loadings.T, sample_rows.T

    return local


def solution(mesh):
    samp, var = mesh.shape["samp"], mesh.shape["var"]

    def whole(genotypes, frequency, start_block):
        cols = start_block.shape[0] // var
        if samp == 16 and var == 2 and cols % (samp * LANES) == 0:
            local = make_local(samp // 4, var)
        else:
            local = make_plain(samp, var)
        placed = (P("samp", "var"), P("var"), P("var", None))
        return jax.shard_map(
            local, mesh=mesh, in_specs=placed, out_specs=(P("var", None), P("samp", None)), check_vma=False
        )(genotypes, frequency, start_block)

    return whole
```
